512 devices in a mesh: ctx: 64 (over z, x, y_hi), head: 8 (over y_lo, core).
Axes of the slice: x: 4, y: 8 (y_hi: 2, y_lo: 4; y = y_hi * 4 + y_lo), z: 8, core: 2. Of those that a mesh axis runs over, the one named last changes fastest.
Arguments:
- fresh_query: bfloat16 [1024, 3072], P('ctx', 'head'), may hold values from -64 to 64
- fresh_key: bfloat16 [1024, 3072], P('ctx', 'head'), may hold values from -2.5 to 2.5
- fresh_value: bfloat16 [1024, 3072], P('ctx', 'head'), may hold values from -6 to 6
- cache_key: bfloat16 [65536, 3072], P('ctx', 'head'), may hold values from -6 to 6
- cache_value: bfloat16 [65536, 3072], P('ctx', 'head'), may hold values from -6 to 6
- slot_owner: int32 [64], replicated, may hold values from 0 to 63, each once
- evictor: int32 [1], replicated, may hold values from 0 to 63
- timestep: int32 [1], replicated, may hold values from 0 to 49
- age_slope: float32 [24], P('head'), may hold values from 0.5 to 4
- time_gate: float32 [50, 3072], P(None, 'head'), may hold values from 0.5 to 2
Outputs:
- attn_output: bfloat16 [1024, 3072], P('ctx', 'head')
- next_key: bfloat16 [65536, 3072], P('ctx', 'head')
- next_value: bfloat16 [65536, 3072], P('ctx', 'head')
The draws below stay inside these ranges and needn't reach their ends.
Inputs may be any that keep to these rules, and one draw needn't show every extreme that they name: `slot_owner`: a permutation of the 64 owners.
All inputs are finite; a program needn't handle non-finite values.
Results may differ from the reference program's by a relative error of at most 0.003.
Values may be sent and summed in bfloat16 or wider, within the bound.
No kernel may reach another device: no remote copies, remote signals or barrier semaphores. Data moves between devices by JAX's collectives and lax.ppermute only.
A program may use at most 64 MiB of HBM per device.

```python
import math
import jax
import jax.numpy as jnp
from jax import lax

HEAD_DIM = 128
TIMESTEPS = 50
FRESH_DEV = 16
HEADS = 24
FRESH = 1024
CACHE_DEV = 1024
CACHED = 65536
N_CTX = 64


def fresh_base(key):
    return jnp.clip(jax.random.normal(key, (FRESH, HEADS * HEAD_DIM), jnp.float32), -2.5, 2.5)


def draw_fresh_query(key, part):
    key = jax.random.fold_in(key, 11)
    return jnp.clip(3.0 * jax.random.normal(key, (FRESH, HEADS * HEAD_DIM), jnp.float32), -12.0, 12.0).astype(jnp.bfloat16)


def draw_fresh_key(key, part):
    base = fresh_base(key)
    return base.astype(jnp.bfloat16)


def block_levels(key, shape, pieces, least, largest):
    gain, own = 1.0, jax.random.fold_in(key, 6)
    for axis_at, parts in pieces:
        steps = jnp.exp(jax.random.uniform(jax.random.fold_in(own, axis_at), (parts,), jnp.float32, least / len(pieces), largest / len(pieces)))
        gain = gain * jnp.repeat(steps, shape[axis_at] // parts).reshape([-1 if axis == axis_at else 1 for axis in range(len(shape))])
    return gain


def bell_draw(stream_key, dims, width, most, cuts=(), held_as=jnp.bfloat16):
    level = block_levels(stream_key, dims, cuts, -0.22, 0.18) if cuts else 1.0
    entries = jax.random.normal(stream_key, dims, jnp.float32) * width * level
    return jnp.minimum(jnp.maximum(entries, -most), most).astype(held_as)


def setup_inputs(seed: int = 0) -> dict:
    keys = jax.random.split(jax.random.key(seed), 11)
    return {
        "fresh_query": draw_fresh_query(jax.random.fold_in(keys[10], 71), 0),
        "fresh_key": draw_fresh_key(jax.random.fold_in(keys[10], 71), 0),
        "fresh_value": bell_draw(keys[2], (FRESH, HEADS * HEAD_DIM), 1.0, 6.0, ((0, 64), (1, 8))),
        "cache_key": bell_draw(keys[3], (CACHED, HEADS * HEAD_DIM), 1.0, 6.0, ((0, 64), (1, 8))),
        "cache_value": bell_draw(keys[4], (CACHED, HEADS * HEAD_DIM), 1.0, 6.0, ((0, 64), (1, 8))),
        "slot_owner": jax.random.permutation(keys[5], N_CTX).astype(jnp.int32),
        "evictor": jax.random.randint(keys[6], (1,), 0, N_CTX).astype(jnp.int32),
        "timestep": jax.random.randint(keys[7], (1,), 0, TIMESTEPS).astype(jnp.int32),
        "age_slope": jnp.clip(jnp.exp(math.log(4.0) - 2.0794415 * jax.random.uniform(keys[8], (HEADS,), jnp.float32) ** block_levels(keys[8], (HEADS,), ((0, 8),), -0.2, 0.2)), 0.5, 4.0),
        "time_gate": jnp.clip(0.5 + 1.5 * jax.random.uniform(keys[9], (TIMESTEPS, HEADS * HEAD_DIM), jnp.float32) ** block_levels(keys[9], (TIMESTEPS, HEADS * HEAD_DIM), ((1, 8),), -0.2, 0.2), 0.5, 2.0),
    }


def reference(fresh_query, fresh_key, fresh_value, cache_key, cache_value, slot_owner, evictor, timestep, age_slope, time_gate):
    owner_ids = jnp.arange(N_CTX, dtype=jnp.int32)
    slot_rank = lax.optimization_barrier(jnp.sum(jnp.where(slot_owner[None, :] == owner_ids[:, None], owner_ids[None, :], 0), axis=1))
    cache_age = (slot_rank + 1).astype(jnp.float32) / N_CTX
    key_age = jnp.concatenate([jnp.zeros((FRESH,), jnp.float32), jnp.repeat(cache_age, CACHE_DEV)])
    all_keys = jnp.concatenate([fresh_key, cache_key], 0).reshape(-1, HEADS, HEAD_DIM).transpose(1, 0, 2)
    all_values = jnp.concatenate([fresh_value, cache_value], 0).reshape(-1, HEADS, HEAD_DIM).transpose(1, 0, 2)
    queries = fresh_query.reshape(FRESH, HEADS, HEAD_DIM).transpose(1, 0, 2)
    score_scale = 1.0 / math.sqrt(HEAD_DIM)

    def group_terms(part_scores, group_max, part_values):
        rounded = lax.optimization_barrier(jnp.exp(part_scores - group_max[:, :, None]).astype(jnp.bfloat16))
        weights = rounded.astype(jnp.float32)
        den = lax.optimization_barrier(jnp.sum(weights, axis=2))
        num = jnp.einsum('ink,nkd->ind', weights, part_values, precision=lax.Precision.HIGHEST)
        return (num, den)

    def one_head(head_args):
        head_query, head_keys, head_values, slope = head_args
        scores = jnp.dot(head_query.astype(jnp.float32), head_keys.astype(jnp.float32).T, precision=lax.Precision.HIGHEST) * score_scale - slope * key_age[None, :]
        fresh_scores = scores[:, :FRESH].reshape(FRESH, N_CTX, FRESH_DEV)
        cache_scores = scores[:, FRESH:].reshape(FRESH, N_CTX, CACHE_DEV)
        values32 = head_values.astype(jnp.float32)
        fresh_vals = values32[:FRESH].reshape(N_CTX, FRESH_DEV, HEAD_DIM)
        cache_vals = values32[FRESH:].reshape(N_CTX, CACHE_DEV, HEAD_DIM)
        group_max = jnp.maximum(lax.optimization_barrier(jnp.max(fresh_scores, axis=2)), lax.optimization_barrier(jnp.max(cache_scores, axis=2)))
        num_a, den_a = group_terms(fresh_scores, group_max, fresh_vals)
        num_b, den_b = group_terms(cache_scores, group_max, cache_vals)
        row_max = lax.optimization_barrier(jnp.max(group_max, axis=1, keepdims=True))
        factor = jnp.exp(group_max - row_max)
        numerator = lax.optimization_barrier(jnp.sum(factor[:, :, None] * (num_a + num_b), axis=1))
        denominator = lax.optimization_barrier(jnp.sum(factor * (den_a + den_b), axis=1))
        return numerator / denominator[:, None]
    attended = lax.map(one_head, (queries, all_keys, all_values, age_slope))
    attended = attended.transpose(1, 0, 2).reshape(FRESH, HEADS * HEAD_DIM)
    squares = lax.optimization_barrier(jnp.sum(attended * attended, axis=1))
    inverse = lax.rsqrt(squares / (HEADS * HEAD_DIM) + 1e-06)
    gate_row = time_gate[timestep[0]]
    attn_output = (attended * inverse[:, None] * gate_row[None, :]).astype(jnp.bfloat16)
    start = (evictor[0] * CACHE_DEV).astype(jnp.int32)
    next_key = lax.dynamic_update_slice_in_dim(cache_key, fresh_key, start, 0)
    next_value = lax.dynamic_update_slice_in_dim(cache_value, fresh_value, start, 0)
    return (attn_output, next_key, next_value)
```

```python
import math

import jax
import jax.numpy as jnp
from jax import lax
from jax.experimental import pallas as pl
from jax.experimental.pallas import tpu as pltpu
from jax.sharding import Mesh, PartitionSpec as P

CTX = ("z", "x", "yh")
PLANE = ("x", "yh")
HEAD = ("yl", "core")
SPLIT = {"z": 8, "x": 4, "yh": 2, "yl": 4, "core": 2}
OWNERS = 64
ROWS = 16
HEADS = 3
DIM = 128
WIDTH = HEADS * DIM
TOKENS = OWNERS * ROWS
CACHE = 1024
BLOCK = 256
SENDERS = BLOCK // ROWS
MSG_ROWS = HEADS * ROWS + 8
FEATURES = 3072
LOG2E = math.log2(math.e)
SCALE2 = LOG2E / math.sqrt(DIM)
F32 = jnp.float32
BF16 = jnp.bfloat16


def dot_nt(a, b):
    return lax.dot_general(a, b, (((1,), (1,)), ((), ())), preferred_element_type=F32)


def softmax_part(query, key, value):
    scores = dot_nt(query, key)
    largest = jnp.max(scores, axis=1, keepdims=True)
    weights = jnp.exp2((scores - largest) * SCALE2).astype(BF16)
    with_ones = jnp.concatenate([value, jnp.ones_like(value)], axis=1)
    both = jnp.dot(weights, with_ones, preferred_element_type=F32)
    total = both[:, DIM:]
    return both[:, :DIM] / total, largest * SCALE2 + jnp.log2(total)


def attend_kernel(owner_ref, slope_ref, q_ref, k_ref, v_ref, slots_ref, msg_ref, nk_ref, nv_ref, sem):
    step = pl.program_id(0)
    copies = [
        pltpu.make_async_copy(k_ref, nk_ref, sem.at[0]),
        pltpu.make_async_copy(v_ref, nv_ref, sem.at[1]),
    ]

    @pl.when(step == 0)
    def _():
        for copy in copies:
            copy.start()

    slots = slots_ref[...]
    slot_ids = lax.broadcasted_iota(jnp.int32, slots.shape, 1)
    rank = jnp.sum(jnp.where(slots == owner_ref[0], slot_ids, 0).astype(F32), axis=1, keepdims=True)
    age = (rank + 1.0) / OWNERS
    lane = lax.broadcasted_iota(jnp.int32, (BLOCK, DIM), 1)
    piece = lane % 64
    stats = jnp.zeros((BLOCK, DIM), F32)
    for h in range(HEADS):
        cols = slice(h * DIM, (h + 1) * DIM)
        part, weight = softmax_part(q_ref[:, cols], k_ref[:, cols], v_ref[:, cols])
        weight = weight - age * (slope_ref[h] * LOG2E)
        msg_ref[:, h * ROWS : (h + 1) * ROWS, :] = part.astype(BF16).reshape(SENDERS, ROWS, DIM)
        for at in (0, 8, 16):
            rounded = weight.astype(BF16).astype(F32)
            stats = jnp.where(piece == at + h, rounded, stats)
            weight = weight - rounded
    halves = stats.reshape(SENDERS, 2, 8, DIM)
    first = lax.broadcasted_iota(jnp.int32, (SENDERS, 8, DIM), 2) < 64
    msg_ref[:, HEADS * ROWS :, :] = jnp.where(first, halves[:, 0], halves[:, 1]).astype(BF16)

    @pl.when(step == pl.num_programs(0) - 1)
    def _():
        for copy in copies:
            copy.wait()


def attend(owner, slope, query, key, value, slots):
    whole = lambda shape: pl.BlockSpec(shape, lambda i: (0,) * len(shape))
    return pl.pallas_call(
        attend_kernel,
        grid=(TOKENS // BLOCK,),
        in_specs=[
            pl.BlockSpec(memory_space=pltpu.SMEM),
            pl.BlockSpec(memory_space=pltpu.SMEM),
            pl.BlockSpec((BLOCK, WIDTH), lambda i: (i, 0)),
            whole((CACHE, WIDTH)),
            whole((CACHE, WIDTH)),
            whole((1, OWNERS)),
        ],
        out_specs=[
            pl.BlockSpec((SENDERS, MSG_ROWS, DIM), lambda i: (i, 0, 0)),
            pl.BlockSpec(memory_space=pl.ANY),
            pl.BlockSpec(memory_space=pl.ANY),
        ],
        out_shape=[
            jax.ShapeDtypeStruct((OWNERS, MSG_ROWS, DIM), BF16),
            jax.ShapeDtypeStruct((CACHE, WIDTH), BF16),
            jax.ShapeDtypeStruct((CACHE, WIDTH), BF16),
        ],
        scratch_shapes=[pltpu.SemaphoreType.DMA((2,))],
        compiler_params=pltpu.CompilerParams(vmem_limit_bytes=48 * 2**20),
        name="attend",
    )(owner, slope, query, key, value, slots)


def merge_kernel(owner_ref, evictor_ref, time_ref, q_ref, kv_ref, msg_ref, gate_ref, nk_in, nv_in, gated_ref, square_ref, nk_ref, nv_ref, sem):
    evicted = owner_ref[0] == evictor_ref[0]
    copies = [
        pltpu.make_async_copy(kv_ref.at[:, :WIDTH], nk_ref, sem.at[0]),
        pltpu.make_async_copy(kv_ref.at[:, WIDTH:], nv_ref, sem.at[1]),
    ]

    @pl.when(evicted)
    def _():
        for copy in copies:
            copy.start()

    lane = lax.broadcasted_iota(jnp.int32, (8, DIM), 1)
    fresh_parts = []
    fresh_weight = jnp.full((8, DIM), 0.0, F32)
    for h in range(HEADS):
        cols = slice(h * DIM, (h + 1) * DIM)
        vcols = slice(WIDTH + h * DIM, WIDTH + (h + 1) * DIM)
        part, weight = softmax_part(q_ref[:, cols], kv_ref[:, cols], kv_ref[:, vcols])
        fresh_parts.append(part)
        fresh_weight = jnp.where(lane == h, weight[:8], fresh_weight)
        fresh_weight = jnp.where(lane == 64 + h, weight[8:], fresh_weight)

    pieces = msg_ref[:, HEADS * ROWS :, :].astype(F32).reshape(OWNERS * 8, DIM)
    weights = pieces + pltpu.roll(pieces, DIM - 8, 1) + pltpu.roll(pieces, DIM - 16, 1)
    weights = weights.reshape(OWNERS, 8, DIM)
    largest = jnp.maximum(jnp.max(weights, axis=0), fresh_weight)
    factor = jnp.exp2(weights - largest[None])
    fresh_factor = jnp.exp2(fresh_weight - largest)
    total = jnp.sum(factor, axis=0) + fresh_factor
    squares = jnp.zeros((ROWS, 1), F32)
    picked = lax.broadcasted_iota(jnp.int32, (gate_ref.shape[0], DIM), 0) == time_ref[0]
    for h in range(HEADS):
        cols = slice(h * DIM, (h + 1) * DIM)
        parts = msg_ref[:, h * ROWS : (h + 1) * ROWS, :].astype(F32).reshape(OWNERS, 2, 8, DIM)
        halves = []
        for half in range(2):
            at = half * 64 + h
            summed = jnp.sum(factor[:, :, at : at + 1] * parts[:, half], axis=0)
            summed += fresh_factor[:, at : at + 1] * fresh_parts[h][half * 8 : half * 8 + 8]
            halves.append(summed / total[:, at : at + 1])
        attended = jnp.concatenate(halves, axis=0)
        squares += jnp.sum(attended * attended, axis=1, keepdims=True)
        gate = jnp.sum(jnp.where(picked, gate_ref[:, cols], 0.0), axis=0, keepdims=True)
        gated_ref[:, cols] = attended * gate
    row = lax.broadcasted_iota(jnp.int32, (ROWS, DIM), 0)
    column = lax.broadcasted_iota(jnp.int32, (ROWS, DIM), 1)
    line = jnp.sum(jnp.where(row == column, squares, 0.0), axis=0, keepdims=True)
    square_ref[...] = jnp.broadcast_to(line[None], square_ref.shape)

    @pl.when(evicted)
    def _():
        for copy in copies:
            copy.wait()


def merge(owner, evictor, timestep, query, kv, msg, gate, next_key, next_value):
    smem = pl.BlockSpec(memory_space=pltpu.SMEM)
    vmem = pl.BlockSpec(memory_space=pltpu.VMEM)
    hbm = pl.BlockSpec(memory_space=pl.ANY)
    return pl.pallas_call(
        merge_kernel,
        in_specs=[smem, smem, smem, vmem, vmem, vmem, vmem, hbm, hbm],
        out_specs=[vmem, vmem, hbm, hbm],
        out_shape=[
            jax.ShapeDtypeStruct((ROWS, WIDTH), F32),
            jax.ShapeDtypeStruct((8, 1, DIM), F32),
            jax.ShapeDtypeStruct((CACHE, WIDTH), BF16),
            jax.ShapeDtypeStruct((CACHE, WIDTH), BF16),
        ],
        input_output_aliases={7: 2, 8: 3},
        scratch_shapes=[pltpu.SemaphoreType.DMA((2,))],
        compiler_params=pltpu.CompilerParams(vmem_limit_bytes=48 * 2**20),
        name="merge",
    )(owner, evictor, timestep, query, kv, msg, gate, next_key, next_value)


def finish_kernel(gated_ref, square_ref, out_ref):
    line = jnp.sum(square_ref[...], axis=0)
    row = lax.broadcasted_iota(jnp.int32, (ROWS, DIM), 0)
    column = lax.broadcasted_iota(jnp.int32, (ROWS, DIM), 1)
    squares = jnp.sum(jnp.where(row == column, line, 0.0), axis=1, keepdims=True)
    out_ref[...] = (gated_ref[...] * lax.rsqrt(squares / FEATURES + 1e-06)).astype(BF16)


def spread(block, axis):
    copies = math.prod(SPLIT[name] for name in (axis if isinstance(axis, tuple) else (axis,)))
    sent = jnp.broadcast_to(block[None], (copies,) + block.shape)
    return lax.all_to_all(sent, axis, 0, 0, tiled=True)


def body(
    fresh_query,
    fresh_key,
    fresh_value,
    cache_key,
    cache_value,
    slot_owner,
    evictor,
    timestep,
    age_slope,
    time_gate,
):
    owner = lax.axis_index(CTX).astype(jnp.int32).reshape(1)
    fresh = jnp.concatenate([fresh_query, fresh_key, fresh_value], axis=1)
    plane = spread(fresh, PLANE).reshape(-1, 3 * WIDTH)
    kv = lax.all_gather(plane[:, WIDTH:], "z", axis=0, tiled=True)
    queries = spread(plane[:, :WIDTH], "z").reshape(TOKENS, WIDTH)
    msg, next_key, next_value = attend(
        owner, age_slope, queries, cache_key, cache_value, slot_owner.reshape(1, OWNERS)
    )
    msg = lax.all_to_all(msg, CTX, 0, 0, tiled=True)
    gated, squares, next_key, next_value = merge(
        owner, evictor, timestep, fresh_query, kv, msg, time_gate, next_key, next_value
    )
    squares = lax.all_to_all(squares, HEAD, 0, 0, tiled=True)
    attn_output = pl.pallas_call(
        finish_kernel,
        out_shape=jax.ShapeDtypeStruct((ROWS, WIDTH), BF16),
        name="finish",
    )(gated, squares)
    return attn_output, next_key, next_value


def solution(mesh):
    split = Mesh(mesh.devices.reshape(tuple(SPLIT.values())), tuple(SPLIT))
    both = P(CTX, HEAD)
    return jax.shard_map(
        body,
        mesh=split,
        in_specs=(both,) * 5 + (P(), P(), P(), P(HEAD), P(None, HEAD)),
        out_specs=(both, both, both),
        check_vma=False,
    )
```

```python
import math

import jax
import jax.numpy as jnp
from jax import lax
from jax.experimental import pallas as pl
from jax.experimental.pallas import tpu as pltpu
from jax.sharding import Mesh, PartitionSpec as P

CTX = ("z", "x", "yh")
SHEET = ("z", "yh")
HEAD = ("yl", "core")
SPLIT = {"z": 8, "x": 4, "yh": 2, "yl": 4, "core": 2}
OWNERS = 64
ROWS = 16
HEADS = 3
DIM = 128
WIDTH = HEADS * DIM
TOKENS = OWNERS * ROWS
CACHE = 1024
BLOCK = 1024
SENDERS = BLOCK // ROWS
MSG_ROWS = HEADS * ROWS + 8
FEATURES = 3072
TOP = 32000.0
LOG2E = math.log2(math.e)
SCALE2 = LOG2E / math.sqrt(DIM)
F32 = jnp.float32
BF16 = jnp.bfloat16
I16 = jnp.int16
I32 = jnp.int32


def dot_nt(a, b):
    return lax.dot_general(a, b, (((1,), (1,)), ((), ())), preferred_element_type=F32)


def with_ones(value):
    return jnp.concatenate([value, jnp.ones_like(value)], axis=1)


def softmax_part(query, key, value, fresh_key, fresh_value, penalty):
    cached = dot_nt(query, key)
    fresh = dot_nt(query, fresh_key)
    largest = jnp.maximum(
        jnp.max(cached, axis=1, keepdims=True) * SCALE2 - penalty,
        jnp.max(fresh, axis=1, keepdims=True) * SCALE2,
    )
    cached_weights = jnp.exp2(cached * SCALE2 - (largest + penalty)).astype(BF16)
    fresh_weights = jnp.exp2(fresh * SCALE2 - largest).astype(BF16)
    both = jnp.dot(cached_weights, with_ones(value), preferred_element_type=F32)
    both += jnp.dot(fresh_weights, with_ones(fresh_value), preferred_element_type=F32)
    total = both[:, DIM:]
    return both[:, :DIM] / total, largest + jnp.log2(total)


def attend_kernel(owner_ref, slope_ref, q_ref, k_ref, v_ref, fk_ref, fv_ref, slots_ref, msg_ref, nk_ref, nv_ref, sem):
    step = pl.program_id(0)
    copies = [
        pltpu.make_async_copy(k_ref, nk_ref, sem.at[0]),
        pltpu.make_async_copy(v_ref, nv_ref, sem.at[1]),
    ]

    @pl.when(step == 0)
    def _():
        for copy in copies:
            copy.start()

    slots = slots_ref[...]
    slot_ids = lax.broadcasted_iota(I32, slots.shape, 1)
    rank = jnp.sum(jnp.where(slots == owner_ref[0], slot_ids, 0).astype(F32), axis=1, keepdims=True)
    age = (rank + 1.0) / OWNERS
    piece = lax.broadcasted_iota(I32, (BLOCK, DIM), 1) % 64
    stats = jnp.zeros((BLOCK, DIM), I32)
    for h in range(HEADS):
        cols = slice(h * DIM, (h + 1) * DIM)
        part, weight = softmax_part(
            q_ref[:, cols],
            k_ref[:, cols],
            v_ref[:, cols],
            fk_ref[:, cols],
            fv_ref[:, cols],
            age * (slope_ref[h] * LOG2E),
        )
        reach = jnp.max(jnp.abs(part), axis=1, keepdims=True)
        power = jnp.floor(jnp.log2(jnp.maximum(reach, 1e-30))) + 1.0
        codes = jnp.round(part * (jnp.exp2(-power) * TOP)).astype(I32)
        msg_ref[:, h * ROWS : (h + 1) * ROWS, :] = codes.astype(I16).reshape(SENDERS, ROWS, DIM)
        fixed = jnp.round(weight * 65536.0).astype(I32)
        high = (fixed + 32768) >> 16
        low = fixed - (high << 16)
        stats = jnp.where(piece == h, high, stats)
        stats = jnp.where(piece == 8 + h, low, stats)
        stats = jnp.where(piece == 16 + h, power.astype(I32), stats)
    halves = stats.reshape(SENDERS, 2, 8, DIM)
    early = lax.broadcasted_iota(I32, (SENDERS, 8, DIM), 2) < 64
    packed = jnp.where(early, halves[:, 0], halves[:, 1])
    msg_ref[:, HEADS * ROWS :, :] = packed.astype(I16)

    @pl.when(step == pl.num_programs(0) - 1)
    def _():
        for copy in copies:
            copy.wait()


def attend(owner, slope, query, key, value, fresh_key, fresh_value, slots):
    smem = pl.BlockSpec(memory_space=pltpu.SMEM)
    hbm = pl.BlockSpec(memory_space=pl.ANY)
    whole = lambda shape: pl.BlockSpec(shape, lambda i: (0,) * len(shape))
    pairs = TOKENS * (CACHE + ROWS) * HEADS
    return pl.pallas_call(
        attend_kernel,
        grid=(TOKENS // BLOCK,),
        in_specs=[
            smem,
            smem,
            pl.BlockSpec((BLOCK, WIDTH), lambda i: (i, 0)),
            whole((CACHE, WIDTH)),
            whole((CACHE, WIDTH)),
            whole((ROWS, WIDTH)),
            whole((ROWS, WIDTH)),
            whole((1, OWNERS)),
        ],
        out_specs=[pl.BlockSpec((SENDERS, MSG_ROWS, DIM), lambda i: (i, 0, 0)), hbm, hbm],
        out_shape=[jax.ShapeDtypeStruct((OWNERS, MSG_ROWS, DIM), I16)]
        + [jax.ShapeDtypeStruct((CACHE, WIDTH), BF16)] * 2,
        scratch_shapes=[pltpu.SemaphoreType.DMA((2,))],
        cost_estimate=pl.CostEstimate(
            flops=6 * DIM * pairs, bytes_accessed=4 * CACHE * WIDTH, transcendentals=pairs
        ),
        compiler_params=pltpu.CompilerParams(vmem_limit_bytes=40 * 2**20),
        name="attend",
    )(owner, slope, query, key, value, fresh_key, fresh_value, slots)


def merge_kernel(time_ref, msg_ref, gate_ref, gated_ref, square_ref):
    stats = msg_ref[:, HEADS * ROWS :, :].astype(I32).astype(F32).reshape(OWNERS * 8, DIM)
    weights = stats + pltpu.roll(stats, DIM - 8, 1) * (1.0 / 65536.0)
    powers = pltpu.roll(stats, DIM - 16, 1).reshape(OWNERS, 8, DIM)
    weights = weights.reshape(OWNERS, 8, DIM)
    largest = jnp.max(weights, axis=0)
    factor = jnp.exp2(weights - largest[None])
    total = jnp.sum(factor, axis=0)
    factor = factor * jnp.exp2(powers)
    squares = jnp.zeros((ROWS, 1), F32)
    picked = lax.broadcasted_iota(I32, (gate_ref.shape[0], DIM), 0) == time_ref[0]
    for h in range(HEADS):
        cols = slice(h * DIM, (h + 1) * DIM)
        codes = msg_ref[:, h * ROWS : (h + 1) * ROWS, :]
        parts = codes.astype(I32).astype(F32).reshape(OWNERS, 2, 8, DIM)
        halves = []
        for half in range(2):
            at = half * 64 + h
            summed = jnp.sum(factor[:, :, at : at + 1] * parts[:, half], axis=0)
            halves.append(summed / (total[:, at : at + 1] * TOP))
        attended = jnp.concatenate(halves, axis=0)
        squares += jnp.sum(attended * attended, axis=1, keepdims=True)
        gate = jnp.sum(jnp.where(picked, gate_ref[:, cols], 0.0), axis=0, keepdims=True)
        gated_ref[:, cols] = attended * gate
    row = lax.broadcasted_iota(I32, (ROWS, DIM), 0)
    column = lax.broadcasted_iota(I32, (ROWS, DIM), 1)
    line = jnp.sum(jnp.where(row == column, squares, 0.0), axis=0, keepdims=True)
    square_ref[...] = jnp.broadcast_to(line[None], square_ref.shape)


def merge(timestep, msg, gate):
    smem = pl.BlockSpec(memory_space=pltpu.SMEM)
    vmem = pl.BlockSpec(memory_space=pltpu.VMEM)
    return pl.pallas_call(
        merge_kernel,
        in_specs=[smem, vmem, vmem],
        out_specs=[vmem, vmem],
        out_shape=[
            jax.ShapeDtypeStruct((ROWS, WIDTH), F32),
            jax.ShapeDtypeStruct((8, 1, DIM), F32),
        ],
        compiler_params=pltpu.CompilerParams(vmem_limit_bytes=40 * 2**20),
        name="merge",
    )(timestep, msg, gate)


def evict_kernel(owner_ref, evictor_ref, kv_ref, nk_in, nv_in, nk_ref, nv_ref, held, sem):
    @pl.when(owner_ref[0] == evictor_ref[0])
    def _():
        fetch = pltpu.make_async_copy(kv_ref, held, sem.at[0])
        fetch.start()
        fetch.wait()
        copies = []
        for x in range(SPLIT["x"]):
            for half, out_ref in enumerate((nk_ref, nv_ref)):
                copies.append(
                    pltpu.make_async_copy(
                        held.at[x, :, :, half * WIDTH : (half + 1) * WIDTH],
                        out_ref.at[:, x],
                        sem.at[1 + 2 * x + half],
                    )
                )
        for copy in copies:
            copy.start()
        for copy in copies:
            copy.wait()


def evict(owner, evictor, kv, next_key, next_value):
    smem = pl.BlockSpec(memory_space=pltpu.SMEM)
    hbm = pl.BlockSpec(memory_space=pl.ANY)
    rows = SPLIT["yh"] * ROWS
    gathered = (SPLIT["x"], SPLIT["z"], rows, 2 * WIDTH)
    cached = (SPLIT["z"], SPLIT["x"], rows, WIDTH)
    shape = jax.ShapeDtypeStruct(cached, BF16)
    outs = pl.pallas_call(
        evict_kernel,
        in_specs=[smem, smem, hbm, hbm, hbm],
        out_specs=[hbm, hbm],
        out_shape=[shape, shape],
        input_output_aliases={3: 0, 4: 1},
        scratch_shapes=[
            pltpu.VMEM(gathered, BF16),
            pltpu.SemaphoreType.DMA((1 + 2 * SPLIT["x"],)),
        ],
        compiler_params=pltpu.CompilerParams(vmem_limit_bytes=60 * 2**20),
        name="evict",
    )(owner, evictor, kv.reshape(gathered), next_key.reshape(cached), next_value.reshape(cached))
    return [out.reshape(CACHE, WIDTH) for out in outs]


def spread(block, axis):
    copies = math.prod(SPLIT[name] for name in (axis if isinstance(axis, tuple) else (axis,)))
    sent = jnp.broadcast_to(block[None], (copies,) + block.shape)
    return lax.all_to_all(sent, axis, 0, 0, tiled=True)


def body(
    fresh_query,
    fresh_key,
    fresh_value,
    cache_key,
    cache_value,
    slot_owner,
    evictor,
    timestep,
    age_slope,
    time_gate,
):
    owner = lax.axis_index(CTX).astype(I32).reshape(1)
    fresh = jnp.concatenate([fresh_query, fresh_key, fresh_value], axis=1)
    sheet = spread(fresh, SHEET).reshape(-1, 3 * WIDTH)
    kv = lax.all_gather(sheet[:, WIDTH:], "x", axis=0, tiled=True)
    queries = spread(sheet[:, :WIDTH], "x").reshape(TOKENS, WIDTH)
    msg, next_key, next_value = attend(
        owner, age_slope, queries, cache_key, cache_value, fresh_key, fresh_value, slot_owner.reshape(1, OWNERS)
    )
    msg = lax.all_to_all(msg, ("x",) + SHEET, 0, 0, tiled=True)
    gated, squares = merge(timestep, msg, time_gate)
    squares = lax.all_to_all(squares, HEAD, 0, 0, tiled=True)
    next_key, next_value = evict(owner, evictor, kv, next_key, next_value)
    squares = jnp.sum(squares, axis=(0, 1))[:ROWS, None]
    attn_output = (gated * lax.rsqrt(squares / FEATURES + 1e-06)).astype(BF16)
    return attn_output, next_key, next_value


def solution(mesh):
    split = Mesh(mesh.devices.reshape(tuple(SPLIT.values())), tuple(SPLIT))
    both = P(CTX, HEAD)
    return jax.shard_map(
        body,
        mesh=split,
        in_specs=(both,) * 5 + (P(), P(), P(), P(HEAD), P(None, HEAD)),
        out_specs=(both, both, both),
        check_vma=False,
    )
```

```python
import math

import jax
import jax.numpy as jnp
from jax import lax
from jax.experimental import pallas as pl
from jax.experimental.pallas import tpu as pltpu
from jax.sharding import Mesh, PartitionSpec as P

CTX = ("z", "x", "yh")
SHEET = ("z", "yh")
HEAD = ("yl", "core")
SPLIT = {"z": 8, "x": 4, "yh": 2, "yl": 4, "core": 2}
OWNERS = 64
ROWS = 16
HEADS = 3
DIM = 128
WIDTH = HEADS * DIM
TOKENS = OWNERS * ROWS
CACHE = 1024
BLOCK = 1024
SENDERS = BLOCK // ROWS
TURNS = (0, 1, 3, 2)
MSG_ROWS = HEADS * ROWS + 8
FEATURES = 3072
TOP = 32000.0
LOG2E = math.log2(math.e)
SCALE2 = LOG2E / math.sqrt(DIM)
F32 = jnp.float32
BF16 = jnp.bfloat16
I16 = jnp.int16
I32 = jnp.int32


def dot_nt(a, b):
    return lax.dot_general(a, b, (((1,), (1,)), ((), ())), preferred_element_type=F32)


def with_ones(value):
    return jnp.concatenate([value, jnp.ones_like(value)], axis=1)


def softmax_part(query, key, value, fresh_key, fresh_value, penalty):
    cached = dot_nt(query, key)
    fresh = dot_nt(query, fresh_key)
    largest = jnp.maximum(
        jnp.max(cached, axis=1, keepdims=True) * SCALE2 - penalty,
        jnp.max(fresh, axis=1, keepdims=True) * SCALE2,
    )
    cached_weights = jnp.exp2(cached * SCALE2 - (largest + penalty)).astype(BF16)
    fresh_weights = jnp.exp2(fresh * SCALE2 - largest).astype(BF16)
    both = jnp.dot(cached_weights, with_ones(value), preferred_element_type=F32)
    both += jnp.dot(fresh_weights, with_ones(fresh_value), preferred_element_type=F32)
    total = both[:, DIM:]
    return both[:, :DIM] / total, largest + jnp.log2(total)


def attend_kernel(owner_ref, slope_ref, q_ref, k_ref, v_ref, fk_ref, fv_ref, slots_ref, msg_ref, nk_ref, nv_ref, sem):
    step = pl.program_id(0)
    copies = [
        pltpu.make_async_copy(k_ref, nk_ref, sem.at[0]),
        pltpu.make_async_copy(v_ref, nv_ref, sem.at[1]),
    ]

    @pl.when(step == 0)
    def _():
        for copy in copies:
            copy.start()

    slots = slots_ref[...]
    slot_ids = lax.broadcasted_iota(I32, slots.shape, 1)
    rank = jnp.sum(jnp.where(slots == owner_ref[0], slot_ids, 0).astype(F32), axis=1, keepdims=True)
    age = (rank + 1.0) / OWNERS
    piece = lax.broadcasted_iota(I32, (BLOCK, DIM), 1) % 64
    stats = jnp.zeros((BLOCK, DIM), I32)
    for h in range(HEADS):
        cols = slice(h * DIM, (h + 1) * DIM)
        part, weight = softmax_part(
            q_ref[:, cols],
            k_ref[:, cols],
            v_ref[:, cols],
            fk_ref[:, cols],
            fv_ref[:, cols],
            age * (slope_ref[h] * LOG2E),
        )
        reach = jnp.max(jnp.abs(part), axis=1, keepdims=True)
        power = jnp.floor(jnp.log2(jnp.maximum(reach, 1e-30))) + 1.0
        codes = jnp.round(part * (jnp.exp2(-power) * TOP)).astype(I32)
        msg_ref[:, h * ROWS : (h + 1) * ROWS, :] = codes.astype(I16).reshape(SENDERS, ROWS, DIM)
        fixed = jnp.round(weight * 65536.0).astype(I32)
        high = (fixed + 32768) >> 16
        low = fixed - (high << 16)
        stats = jnp.where(piece == h, high, stats)
        stats = jnp.where(piece == 8 + h, low, stats)
        stats = jnp.where(piece == 16 + h, power.astype(I32), stats)
    halves = stats.reshape(SENDERS, 2, 8, DIM)
    early = lax.broadcasted_iota(I32, (SENDERS, 8, DIM), 2) < 64
    packed = jnp.where(early, halves[:, 0], halves[:, 1])
    msg_ref[:, HEADS * ROWS :, :] = packed.astype(I16)

    @pl.when(step == pl.num_programs(0) - 1)
    def _():
        for copy in copies:
            copy.wait()


def attend(owner, slope, query, key, value, fresh_key, fresh_value, slots):
    smem = pl.BlockSpec(memory_space=pltpu.SMEM)
    hbm = pl.BlockSpec(memory_space=pl.ANY)
    whole = lambda shape: pl.BlockSpec(shape, lambda i: (0,) * len(shape))
    pairs = TOKENS * (CACHE + ROWS) * HEADS
    return pl.pallas_call(
        attend_kernel,
        grid=(TOKENS // BLOCK,),
        in_specs=[
            smem,
            smem,
            pl.BlockSpec((BLOCK, WIDTH), lambda i: (i, 0)),
            whole((CACHE, WIDTH)),
            whole((CACHE, WIDTH)),
            whole((ROWS, WIDTH)),
            whole((ROWS, WIDTH)),
            whole((1, OWNERS)),
        ],
        out_specs=[pl.BlockSpec((SENDERS, MSG_ROWS, DIM), lambda i: (i, 0, 0)), hbm, hbm],
        out_shape=[jax.ShapeDtypeStruct((OWNERS, MSG_ROWS, DIM), I16)]
        + [jax.ShapeDtypeStruct((CACHE, WIDTH), BF16)] * 2,
        scratch_shapes=[pltpu.SemaphoreType.DMA((2,))],
        cost_estimate=pl.CostEstimate(
            flops=6 * DIM * pairs, bytes_accessed=4 * CACHE * WIDTH, transcendentals=pairs
        ),
        compiler_params=pltpu.CompilerParams(vmem_limit_bytes=40 * 2**20),
        name="attend",
    )(owner, slope, query, key, value, fresh_key, fresh_value, slots)


def merge_kernel(time_ref, msg_ref, gate_ref, gated_ref, square_ref):
    stats = msg_ref[:, HEADS * ROWS :, :].astype(I32).astype(F32).reshape(OWNERS * 8, DIM)
    weights = stats + pltpu.roll(stats, DIM - 8, 1) * (1.0 / 65536.0)
    powers = pltpu.roll(stats, DIM - 16, 1).reshape(OWNERS, 8, DIM)
    weights = weights.reshape(OWNERS, 8, DIM)
    largest = jnp.max(weights, axis=0)
    factor = jnp.exp2(weights - largest[None])
    total = jnp.sum(factor, axis=0)
    factor = factor * jnp.exp2(powers)
    squares = jnp.zeros((ROWS, 1), F32)
    picked = lax.broadcasted_iota(I32, (gate_ref.shape[0], DIM), 0) == time_ref[0]
    for h in range(HEADS):
        cols = slice(h * DIM, (h + 1) * DIM)
        codes = msg_ref[:, h * ROWS : (h + 1) * ROWS, :]
        parts = codes.astype(I32).astype(F32).reshape(OWNERS, 2, 8, DIM)
        halves = []
        for half in range(2):
            at = half * 64 + h
            summed = jnp.sum(factor[:, :, at : at + 1] * parts[:, half], axis=0)
            halves.append(summed / (total[:, at : at + 1] * TOP))
        attended = jnp.concatenate(halves, axis=0)
        squares += jnp.sum(attended * attended, axis=1, keepdims=True)
        gate = jnp.sum(jnp.where(picked, gate_ref[:, cols], 0.0), axis=0, keepdims=True)
        gated_ref[:, cols] = attended * gate
    row = lax.broadcasted_iota(I32, (ROWS, DIM), 0)
    column = lax.broadcasted_iota(I32, (ROWS, DIM), 1)
    line = jnp.sum(jnp.where(row == column, squares, 0.0), axis=0, keepdims=True)
    square_ref[...] = jnp.broadcast_to(line[None], square_ref.shape)


def merge(timestep, msg, gate):
    smem = pl.BlockSpec(memory_space=pltpu.SMEM)
    vmem = pl.BlockSpec(memory_space=pltpu.VMEM)
    return pl.pallas_call(
        merge_kernel,
        in_specs=[smem, vmem, vmem],
        out_specs=[vmem, vmem],
        out_shape=[
            jax.ShapeDtypeStruct((ROWS, WIDTH), F32),
            jax.ShapeDtypeStruct((8, 1, DIM), F32),
        ],
        compiler_params=pltpu.CompilerParams(vmem_limit_bytes=40 * 2**20),
        name="merge",
    )(timestep, msg, gate)


def evict_kernel(owner_ref, evictor_ref, *refs):
    blocks, (nk_ref, nv_ref, held, sem) = refs[: len(TURNS)], refs[-4:]

    @pl.when(owner_ref[0] == evictor_ref[0])
    def _():
        fetches = [
            pltpu.make_async_copy(block, held.at[at], sem.at[at]) for at, block in enumerate(blocks)
        ]
        for fetch in fetches:
            fetch.start()
        for fetch in fetches:
            fetch.wait()
        copies = []
        for at, turn in enumerate(TURNS):
            x = ((owner_ref[0] >> 1) & 3) ^ turn
            for half, out_ref in enumerate((nk_ref, nv_ref)):
                copies.append(
                    pltpu.make_async_copy(
                        held.at[at, :, :, half * WIDTH : (half + 1) * WIDTH],
                        out_ref.at[:, x],
                        sem.at[len(TURNS) + 2 * at + half],
                    )
                )
        for copy in copies:
            copy.start()
        for copy in copies:
            copy.wait()


def evict(owner, evictor, blocks, next_key, next_value):
    smem = pl.BlockSpec(memory_space=pltpu.SMEM)
    hbm = pl.BlockSpec(memory_space=pl.ANY)
    rows = SPLIT["yh"] * ROWS
    gathered = (SPLIT["z"], rows, 2 * WIDTH)
    cached = (SPLIT["z"], SPLIT["x"], rows, WIDTH)
    shape = jax.ShapeDtypeStruct(cached, BF16)
    first = 2 + len(TURNS)
    outs = pl.pallas_call(
        evict_kernel,
        in_specs=[smem, smem] + [hbm] * (len(TURNS) + 2),
        out_specs=[hbm, hbm],
        out_shape=[shape, shape],
        input_output_aliases={first: 0, first + 1: 1},
        scratch_shapes=[
            pltpu.VMEM((len(TURNS),) + gathered, BF16),
            pltpu.SemaphoreType.DMA((3 * len(TURNS),)),
        ],
        compiler_params=pltpu.CompilerParams(vmem_limit_bytes=60 * 2**20),
        name="evict",
    )(
        owner,
        evictor,
        *[block.reshape(gathered) for block in blocks],
        next_key.reshape(cached),
        next_value.reshape(cached),
    )
    return [out.reshape(CACHE, WIDTH) for out in outs]


def pick_kernel(sheet_ref, after_ref, kv_ref):
    kv_ref[...] = sheet_ref[:, WIDTH:]


def pick(sheet, after):
    vmem = pl.BlockSpec(memory_space=pltpu.VMEM)
    return pl.pallas_call(
        pick_kernel,
        in_specs=[vmem, pl.BlockSpec(memory_space=pl.ANY)],
        out_specs=vmem,
        out_shape=jax.ShapeDtypeStruct((sheet.shape[0], 2 * WIDTH), BF16),
        name="pick",
    )(sheet, after)


def spread(block, axis):
    copies = math.prod(SPLIT[name] for name in (axis if isinstance(axis, tuple) else (axis,)))
    sent = jnp.broadcast_to(block[None], (copies,) + block.shape)
    return lax.all_to_all(sent, axis, 0, 0, tiled=True)


def body(
    fresh_query,
    fresh_key,
    fresh_value,
    cache_key,
    cache_value,
    slot_owner,
    evictor,
    timestep,
    age_slope,
    time_gate,
):
    owner = lax.axis_index(CTX).astype(I32).reshape(1)
    fresh = jnp.concatenate([fresh_query, fresh_key, fresh_value], axis=1)
    sheet = spread(fresh, SHEET).reshape(-1, 3 * WIDTH)
    queries = spread(sheet[:, :WIDTH], "x").reshape(TOKENS, WIDTH)
    msg, next_key, next_value = attend(
        owner, age_slope, queries, cache_key, cache_value, fresh_key, fresh_value, slot_owner.reshape(1, OWNERS)
    )
    kv = [pick(sheet, msg)]
    for turn in TURNS[1:]:
        kv.append(lax.ppermute(kv[0], "x", [(i, i ^ turn) for i in range(SPLIT["x"])]))
    msg = lax.all_to_all(msg, ("x",) + SHEET, 0, 0, tiled=True)
    gated, squares = merge(timestep, msg, time_gate)
    squares = lax.all_to_all(squares, HEAD, 0, 0, tiled=True)
    next_key, next_value = evict(owner, evictor, kv, next_key, next_value)
    squares = jnp.sum(squares, axis=(0, 1))[:ROWS, None]
    attn_output = (gated * lax.rsqrt(squares / FEATURES + 1e-06)).astype(BF16)
    return attn_output, next_key, next_value


def solution(mesh):
    split = Mesh(mesh.devices.reshape(tuple(SPLIT.values())), tuple(SPLIT))
    both = P(CTX, HEAD)
    return jax.shard_map(
        body,
        mesh=split,
        in_specs=(both,) * 5 + (P(), P(), P(), P(HEAD), P(None, HEAD)),
        out_specs=(both, both, both),
        check_vma=False,
    )
```

```python
import functools
import math

import jax
import jax.numpy as jnp
from jax import lax
from jax.experimental import pallas as pl
from jax.experimental.pallas import tpu as pltpu
from jax.sharding import Mesh, PartitionSpec as P

CTX = ("z", "x", "yh")
SHEET = ("z", "yh")
HEAD = ("yl", "core")
SPLIT = {"z": 8, "x": 4, "yh": 2, "yl": 4, "core": 2}
OWNERS = 64
ROWS = 16
HEADS = 3
DIM = 128
WIDTH = HEADS * DIM
TOKENS = OWNERS * ROWS
CACHE = 1024
SENDERS = OWNERS // 4
TURNS = (0, 1, 3, 2)
MSG_ROWS = HEADS * ROWS + 8
FEATURES = 3072
TOP = 32000.0
LOG2E = math.log2(math.e)
SCALE2 = LOG2E / math.sqrt(DIM)
F32 = jnp.float32
BF16 = jnp.bfloat16
I16 = jnp.int16
I32 = jnp.int32


def dot_nt(a, b):
    return lax.dot_general(a, b, (((1,), (1,)), ((), ())), preferred_element_type=F32)


def with_ones(value):
    return jnp.concatenate([value, jnp.ones_like(value)], axis=1)


def softmax_part(query, key, value, fresh_key, fresh_value, penalty):
    cached = dot_nt(query, key)
    fresh = dot_nt(query, fresh_key)
    largest = jnp.maximum(
        jnp.max(cached, axis=1, keepdims=True) * SCALE2 - penalty,
        jnp.max(fresh, axis=1, keepdims=True) * SCALE2,
    )
    cached_weights = jnp.exp2(cached * SCALE2 - (largest + penalty)).astype(BF16)
    fresh_weights = jnp.exp2(fresh * SCALE2 - largest).astype(BF16)
    both = jnp.dot(cached_weights, with_ones(value), preferred_element_type=F32)
    both += jnp.dot(fresh_weights, with_ones(fresh_value), preferred_element_type=F32)
    total = both[:, DIM:]
    return both[:, :DIM] / total, largest + jnp.log2(total)


def attend_kernel(turns, owner_ref, slope_ref, k_ref, v_ref, fk_ref, fv_ref, slots_ref, *refs):
    q_refs, (held, sem) = refs[: len(turns)], refs[-2:]
    if turns[0] == 0:
        msg_ref, nk_ref, nv_ref = refs[len(turns) : -2]
        copies = [
            pltpu.make_async_copy(k_ref, nk_ref, sem.at[0]),
            pltpu.make_async_copy(v_ref, nv_ref, sem.at[1]),
        ]
    else:
        msg_ref, copies = refs[-3], []
    for copy in copies:
        copy.start()
    tokens = len(turns) * SENDERS * ROWS
    senders = len(turns) * SENDERS
    slots = slots_ref[...]
    slot_ids = lax.broadcasted_iota(I32, slots.shape, 1)
    rank = jnp.sum(jnp.where(slots == owner_ref[0], slot_ids, 0).astype(F32), axis=1, keepdims=True)
    age = (rank + 1.0) / OWNERS
    piece = lax.broadcasted_iota(I32, (tokens, DIM), 1) % 64
    stats = jnp.zeros((tokens, DIM), I32)
    for h in range(HEADS):
        cols = slice(h * DIM, (h + 1) * DIM)
        part, weight = softmax_part(
            jnp.concatenate([q_ref[:, cols] for q_ref in q_refs], axis=0),
            k_ref[:, cols],
            v_ref[:, cols],
            fk_ref[:, cols],
            fv_ref[:, cols],
            age * (slope_ref[:, h : h + 1] * LOG2E),
        )
        reach = jnp.max(jnp.abs(part), axis=1, keepdims=True)
        power = jnp.floor(jnp.log2(jnp.maximum(reach, 1e-30))) + 1.0
        codes = jnp.round(part * (jnp.exp2(-power) * TOP)).astype(I32)
        held[:, h * ROWS : (h + 1) * ROWS, :] = codes.astype(I16).reshape(senders, ROWS, DIM)
        fixed = jnp.round(weight * 65536.0).astype(I32)
        high = (fixed + 32768) >> 16
        low = fixed - (high << 16)
        stats = jnp.where(piece == h, high, stats)
        stats = jnp.where(piece == 8 + h, low, stats)
        stats = jnp.where(piece == 16 + h, power.astype(I32), stats)
    halves = stats.reshape(senders, 2, 8, DIM)
    early = lax.broadcasted_iota(I32, (senders, 8, DIM), 2) < 64
    packed = jnp.where(early, halves[:, 0], halves[:, 1])
    held[:, HEADS * ROWS :, :] = packed.astype(I16)
    for at, turn in enumerate(turns):
        x = ((owner_ref[0] >> 1) & 3) ^ turn
        copies.append(
            pltpu.make_async_copy(
                held.at[at * SENDERS : (at + 1) * SENDERS],
                msg_ref.at[pl.ds(x * SENDERS, SENDERS)],
                sem.at[2 + at],
            )
        )
        copies[-1].start()

    for copy in copies:
        copy.wait()


def attend(turns, owner, slope, queries, key, value, fresh_key, fresh_value, slots, msg=None):
    vmem = pl.BlockSpec(memory_space=pltpu.VMEM)
    hbm = pl.BlockSpec(memory_space=pl.ANY)
    pairs = len(turns) * SENDERS * ROWS * (CACHE + ROWS) * HEADS
    args = [owner, slope, key, value, fresh_key, fresh_value, slots, *queries]
    in_specs = [pl.BlockSpec(memory_space=pltpu.SMEM)] + [vmem] * (6 + len(turns))
    out_shape = [jax.ShapeDtypeStruct((OWNERS, MSG_ROWS, DIM), I16)]
    aliases = {}
    if msg is None:
        out_shape += [jax.ShapeDtypeStruct((CACHE, WIDTH), BF16)] * 2
    else:
        aliases = {len(args): 0}
        args.append(msg)
        in_specs.append(hbm)
    return pl.pallas_call(
        functools.partial(attend_kernel, turns),
        in_specs=in_specs,
        out_specs=[hbm] * len(out_shape),
        out_shape=out_shape,
        input_output_aliases=aliases,
        scratch_shapes=[
            pltpu.VMEM((len(turns) * SENDERS, MSG_ROWS, DIM), I16),
            pltpu.SemaphoreType.DMA((2 + len(turns),)),
        ],
        cost_estimate=pl.CostEstimate(
            flops=6 * DIM * pairs, bytes_accessed=4 * CACHE * WIDTH, transcendentals=pairs
        ),
        compiler_params=pltpu.CompilerParams(vmem_limit_bytes=40 * 2**20),
        name="attend",
    )(*args)


def merge_kernel(time_ref, msg_ref, gate_ref, gated_ref, square_ref):
    stats = msg_ref[:, HEADS * ROWS :, :].astype(I32).astype(F32).reshape(OWNERS * 8, DIM)
    weights = stats + pltpu.roll(stats, DIM - 8, 1) * (1.0 / 65536.0)
    powers = pltpu.roll(stats, DIM - 16, 1).reshape(OWNERS, 8, DIM)
    weights = weights.reshape(OWNERS, 8, DIM)
    largest = jnp.max(weights, axis=0)
    factor = jnp.exp2(weights - largest[None])
    total = jnp.sum(factor, axis=0)
    factor = factor * jnp.exp2(powers)
    squares = jnp.zeros((ROWS, 1), F32)
    picked = lax.broadcasted_iota(I32, (gate_ref.shape[0], DIM), 0) == time_ref[0]
    for h in range(HEADS):
        cols = slice(h * DIM, (h + 1) * DIM)
        codes = msg_ref[:, h * ROWS : (h + 1) * ROWS, :]
        parts = codes.astype(I32).astype(F32).reshape(OWNERS, 2, 8, DIM)
        halves = []
        for half in range(2):
            at = half * 64 + h
            summed = jnp.sum(factor[:, :, at : at + 1] * parts[:, half], axis=0)
            halves.append(summed / (total[:, at : at + 1] * TOP))
        attended = jnp.concatenate(halves, axis=0)
        squares += jnp.sum(attended * attended, axis=1, keepdims=True)
        gate = jnp.sum(jnp.where(picked, gate_ref[:, cols], 0.0), axis=0, keepdims=True)
        gated_ref[:, cols] = attended * gate
    row = lax.broadcasted_iota(I32, (ROWS, DIM), 0)
    column = lax.broadcasted_iota(I32, (ROWS, DIM), 1)
    line = jnp.sum(jnp.where(row == column, squares, 0.0), axis=0, keepdims=True)
    square_ref[...] = jnp.broadcast_to(line[None], square_ref.shape)


def merge(timestep, msg, gate):
    smem = pl.BlockSpec(memory_space=pltpu.SMEM)
    vmem = pl.BlockSpec(memory_space=pltpu.VMEM)
    return pl.pallas_call(
        merge_kernel,
        in_specs=[smem, vmem, vmem],
        out_specs=[vmem, vmem],
        out_shape=[
            jax.ShapeDtypeStruct((ROWS, WIDTH), F32),
            jax.ShapeDtypeStruct((8, 1, DIM), F32),
        ],
        compiler_params=pltpu.CompilerParams(vmem_limit_bytes=40 * 2**20),
        name="merge",
    )(timestep, msg, gate)


def evict_kernel(owner_ref, evictor_ref, *refs):
    blocks, (nk_ref, nv_ref, held, sem) = refs[: len(TURNS)], refs[-4:]

    @pl.when(owner_ref[0] == evictor_ref[0])
    def _():
        fetches = [
            pltpu.make_async_copy(block, held.at[at], sem.at[at]) for at, block in enumerate(blocks)
        ]
        for fetch in fetches:
            fetch.start()
        for fetch in fetches:
            fetch.wait()
        copies = []
        for at, turn in enumerate(TURNS):
            x = ((owner_ref[0] >> 1) & 3) ^ turn
            for half, out_ref in enumerate((nk_ref, nv_ref)):
                copies.append(
                    pltpu.make_async_copy(
                        held.at[at, :, :, half * WIDTH : (half + 1) * WIDTH],
                        out_ref.at[:, x],
                        sem.at[len(TURNS) + 2 * at + half],
                    )
                )
        for copy in copies:
            copy.start()
        for copy in copies:
            copy.wait()


def evict(owner, evictor, blocks, next_key, next_value):
    smem = pl.BlockSpec(memory_space=pltpu.SMEM)
    hbm = pl.BlockSpec(memory_space=pl.ANY)
    rows = SPLIT["yh"] * ROWS
    gathered = (SPLIT["z"], rows, 2 * WIDTH)
    cached = (SPLIT["z"], SPLIT["x"], rows, WIDTH)
    shape = jax.ShapeDtypeStruct(cached, BF16)
    first = 2 + len(TURNS)
    outs = pl.pallas_call(
        evict_kernel,
        in_specs=[smem, smem] + [hbm] * (len(TURNS) + 2),
        out_specs=[hbm, hbm],
        out_shape=[shape, shape],
        input_output_aliases={first: 0, first + 1: 1},
        scratch_shapes=[
            pltpu.VMEM((len(TURNS),) + gathered, BF16),
            pltpu.SemaphoreType.DMA((3 * len(TURNS),)),
        ],
        compiler_params=pltpu.CompilerParams(vmem_limit_bytes=60 * 2**20),
        name="evict",
    )(
        owner,
        evictor,
        *[block.reshape(gathered) for block in blocks],
        next_key.reshape(cached),
        next_value.reshape(cached),
    )
    return [out.reshape(CACHE, WIDTH) for out in outs]


def pick_kernel(sheet_ref, after_ref, kv_ref):
    kv_ref[...] = sheet_ref[:, WIDTH:]


def pick(sheet, after):
    vmem = pl.BlockSpec(memory_space=pltpu.VMEM)
    return pl.pallas_call(
        pick_kernel,
        in_specs=[vmem, pl.BlockSpec(memory_space=pl.ANY)],
        out_specs=vmem,
        out_shape=jax.ShapeDtypeStruct((sheet.shape[0], 2 * WIDTH), BF16),
        name="pick",
    )(sheet, after)


def spread(block, axis):
    copies = math.prod(SPLIT[name] for name in (axis if isinstance(axis, tuple) else (axis,)))
    sent = jnp.broadcast_to(block[None], (copies,) + block.shape)
    return lax.all_to_all(sent, axis, 0, 0, tiled=True)


def around(block):
    ways = [[(i, i ^ turn) for i in range(SPLIT["x"])] for turn in TURNS[1:]]
    return [block] + [lax.ppermute(block, "x", way) for way in ways]


def body(
    fresh_query,
    fresh_key,
    fresh_value,
    cache_key,
    cache_value,
    slot_owner,
    evictor,
    timestep,
    age_slope,
    time_gate,
):
    owner = lax.axis_index(CTX).astype(I32).reshape(1)
    fresh = jnp.concatenate([fresh_query, fresh_key, fresh_value], axis=1)
    sheet = spread(fresh, SHEET).reshape(-1, 3 * WIDTH)
    queries = around(sheet[:, :WIDTH])
    slope = age_slope.reshape(1, HEADS)
    cache = (cache_key, cache_value, fresh_key, fresh_value, slot_owner.reshape(1, OWNERS))
    msg, next_key, next_value = attend(TURNS[:1], owner, slope, queries[:1], *cache)
    (msg,) = attend(TURNS[1:], owner, slope, queries[1:], *cache, msg)
    kv = around(pick(sheet, msg))
    msg = lax.all_to_all(msg, ("x",) + SHEET, 0, 0, tiled=True)
    gated, squares = merge(timestep, msg, time_gate)
    squares = lax.all_to_all(squares, HEAD, 0, 0, tiled=True)
    next_key, next_value = evict(owner, evictor, kv, next_key, next_value)
    squares = jnp.sum(squares, axis=(0, 1))[:ROWS, None]
    attn_output = (gated * lax.rsqrt(squares / FEATURES + 1e-06)).astype(BF16)
    return attn_output, next_key, next_value


def solution(mesh):
    split = Mesh(mesh.devices.reshape(tuple(SPLIT.values())), tuple(SPLIT))
    both = P(CTX, HEAD)
    return jax.shard_map(
        body,
        mesh=split,
        in_specs=(both,) * 5 + (P(), P(), P(), P(HEAD), P(None, HEAD)),
        out_specs=(both, both, both),
        check_vma=False,
    )
```

```python
import functools
import math

import jax
import jax.numpy as jnp
from jax import lax
from jax.experimental import pallas as pl
from jax.experimental.pallas import tpu as pltpu
from jax.sharding import Mesh, PartitionSpec as P

CTX = ("z", "x", "yh")
SHEET = ("z", "yh")
HEAD = ("yl", "core")
SPLIT = {"z": 8, "x": 4, "yh": 2, "yl": 4, "core": 2}
OWNERS = 64
ROWS = 16
HEADS = 3
DIM = 128
WIDTH = HEADS * DIM
TOKENS = OWNERS * ROWS
CACHE = 1024
SENDERS = OWNERS // 4
TURNS = (0, 1, 3, 2)
MSG_ROWS = HEADS * ROWS + 8
FEATURES = 3072
TOP = 32000.0
LOG2E = math.log2(math.e)
SCALE2 = LOG2E / math.sqrt(DIM)
F32 = jnp.float32
BF16 = jnp.bfloat16
I16 = jnp.int16
I32 = jnp.int32


def dot_nt(a, b):
    return lax.dot_general(a, b, (((1,), (1,)), ((), ())), preferred_element_type=F32)


def with_ones(value):
    return jnp.concatenate([value, jnp.ones_like(value)], axis=1)


def softmax_part(query, key, value, fresh_key, fresh_value, penalty):
    cached = dot_nt(query, key)
    fresh = dot_nt(query, fresh_key)
    largest = jnp.maximum(
        jnp.max(cached, axis=1, keepdims=True) * SCALE2 - penalty,
        jnp.max(fresh, axis=1, keepdims=True) * SCALE2,
    )
    cached_weights = jnp.exp2(cached * SCALE2 - (largest + penalty)).astype(BF16)
    fresh_weights = jnp.exp2(fresh * SCALE2 - largest).astype(BF16)
    both = jnp.dot(cached_weights, with_ones(value), preferred_element_type=F32)
    both += jnp.dot(fresh_weights, with_ones(fresh_value), preferred_element_type=F32)
    total = both[:, DIM:]
    return both[:, :DIM] / total, largest + jnp.log2(total)


def cached_part(query, key, value, penalty):
    scores = dot_nt(query, key)
    largest = jnp.max(scores, axis=1, keepdims=True)
    weights = jnp.exp2((scores - largest) * SCALE2).astype(BF16)
    both = jnp.dot(weights, with_ones(value), preferred_element_type=F32)
    total = both[:, DIM:]
    return both[:, :DIM] / total, largest * SCALE2 - penalty + jnp.log2(total)


def encode(part, weight, h, stats):
    piece = lax.broadcasted_iota(I32, stats.shape, 1) % 64
    reach = jnp.max(jnp.abs(part), axis=1, keepdims=True)
    power = jnp.floor(jnp.log2(jnp.maximum(reach, 1e-30))) + 1.0
    codes = jnp.round(part * (jnp.exp2(-power) * TOP)).astype(I32).astype(I16)
    fixed = jnp.round(weight * 65536.0).astype(I32)
    high = (fixed + 32768) >> 16
    low = fixed - (high << 16)
    stats = jnp.where(piece == h, high, stats)
    stats = jnp.where(piece == 8 + h, low, stats)
    stats = jnp.where(piece == 16 + h, power.astype(I32), stats)
    return codes.reshape(-1, ROWS, DIM), stats


def pack(stats):
    halves = stats.reshape(-1, 2, 8, DIM)
    early = lax.broadcasted_iota(I32, (halves.shape[0], 8, DIM), 2) < 64
    return jnp.where(early, halves[:, 0], halves[:, 1]).astype(I16)


def attend_kernel(turns, owner_ref, slope_ref, k_ref, v_ref, sheet_ref, slots_ref, *refs):
    q_refs, (held, sem) = refs[: len(turns)], refs[-2:]
    if turns[0] == 0:
        msg_ref, nk_ref, nv_ref = refs[len(turns) : -2]
        copies = [
            pltpu.make_async_copy(k_ref, nk_ref, sem.at[0]),
            pltpu.make_async_copy(v_ref, nv_ref, sem.at[1]),
        ]
    else:
        msg_ref, copies = refs[-3], []
    for copy in copies:
        copy.start()
    slots = slots_ref[...]
    slot_ids = lax.broadcasted_iota(I32, slots.shape, 1)
    rank = jnp.sum(jnp.where(slots == owner_ref[0], slot_ids, 0).astype(F32), axis=1, keepdims=True)
    age = (rank + 1.0) / OWNERS
    mine = (owner_ref[0] >> 3) * 2 + (owner_ref[0] & 1)
    rows = pl.ds(pl.multiple_of(mine * ROWS, ROWS), ROWS)
    stats = jnp.zeros((len(turns) * SENDERS * ROWS, DIM), I32)
    few_stats = jnp.zeros((len(turns) * ROWS, DIM), I32)
    for h in range(HEADS):
        cols = slice(h * DIM, (h + 1) * DIM)
        place = slice(h * ROWS, (h + 1) * ROWS)
        penalty = age * (slope_ref[:, h : h + 1] * LOG2E)
        query = jnp.concatenate([q_ref[:, cols] for q_ref in q_refs], axis=0)
        few = jnp.concatenate([q_ref[rows, cols] for q_ref in q_refs], axis=0)
        part, weight = cached_part(query, k_ref[:, cols], v_ref[:, cols], penalty)
        held[:, place, :], stats = encode(part, weight, h, stats)
        new_key = sheet_ref[:, WIDTH + h * DIM : WIDTH + (h + 1) * DIM]
        new_value = sheet_ref[:, 2 * WIDTH + h * DIM : 2 * WIDTH + (h + 1) * DIM]
        part, weight = softmax_part(few, k_ref[:, cols], v_ref[:, cols], new_key, new_value, penalty)
        codes, few_stats = encode(part, weight, h, few_stats)
        for at in range(len(turns)):
            held[at * SENDERS + mine, place, :] = codes[at]
    held[:, HEADS * ROWS :, :] = pack(stats)
    packed = pack(few_stats)
    for at in range(len(turns)):
        held[at * SENDERS + mine, HEADS * ROWS :, :] = packed[at]
    for at, turn in enumerate(turns):
        x = ((owner_ref[0] >> 1) & 3) ^ turn
        copies.append(
            pltpu.make_async_copy(
                held.at[at * SENDERS : (at + 1) * SENDERS],
                msg_ref.at[pl.ds(x * SENDERS, SENDERS)],
                sem.at[2 + at],
            )
        )
        copies[-1].start()

    for copy in copies:
        copy.wait()


def attend(turns, owner, slope, queries, key, value, sheet, slots, msg=None):
    vmem = pl.BlockSpec(memory_space=pltpu.VMEM)
    hbm = pl.BlockSpec(memory_space=pl.ANY)
    pairs = len(turns) * SENDERS * ROWS * (CACHE + ROWS) * HEADS
    args = [owner, slope, key, value, sheet, slots, *queries]
    in_specs = [pl.BlockSpec(memory_space=pltpu.SMEM)] + [vmem] * (5 + len(turns))
    out_shape = [jax.ShapeDtypeStruct((OWNERS, MSG_ROWS, DIM), I16)]
    aliases = {}
    if msg is None:
        out_shape += [jax.ShapeDtypeStruct((CACHE, WIDTH), BF16)] * 2
    else:
        aliases = {len(args): 0}
        args.append(msg)
        in_specs.append(hbm)
    return pl.pallas_call(
        functools.partial(attend_kernel, turns),
        in_specs=in_specs,
        out_specs=[hbm] * len(out_shape),
        out_shape=out_shape,
        input_output_aliases=aliases,
        scratch_shapes=[
            pltpu.VMEM((len(turns) * SENDERS, MSG_ROWS, DIM), I16),
            pltpu.SemaphoreType.DMA((2 + len(turns),)),
        ],
        cost_estimate=pl.CostEstimate(
            flops=6 * DIM * pairs, bytes_accessed=4 * CACHE * WIDTH, transcendentals=pairs
        ),
        compiler_params=pltpu.CompilerParams(vmem_limit_bytes=40 * 2**20),
        name="attend",
    )(*args)


def merge_kernel(time_ref, msg_ref, gate_ref, gated_ref, square_ref):
    stats = msg_ref[:, HEADS * ROWS :, :].astype(I32).astype(F32).reshape(OWNERS * 8, DIM)
    weights = stats + pltpu.roll(stats, DIM - 8, 1) * (1.0 / 65536.0)
    powers = pltpu.roll(stats, DIM - 16, 1).reshape(OWNERS, 8, DIM)
    weights = weights.reshape(OWNERS, 8, DIM)
    largest = jnp.max(weights, axis=0)
    factor = jnp.exp2(weights - largest[None])
    total = jnp.sum(factor, axis=0)
    factor = factor * jnp.exp2(powers)
    squares = jnp.zeros((ROWS, 1), F32)
    picked = lax.broadcasted_iota(I32, (gate_ref.shape[0], DIM), 0) == time_ref[0]
    for h in range(HEADS):
        cols = slice(h * DIM, (h + 1) * DIM)
        codes = msg_ref[:, h * ROWS : (h + 1) * ROWS, :]
        parts = codes.astype(I32).astype(F32).reshape(OWNERS, 2, 8, DIM)
        halves = []
        for half in range(2):
            at = half * 64 + h
            summed = jnp.sum(factor[:, :, at : at + 1] * parts[:, half], axis=0)
            halves.append(summed / (total[:, at : at + 1] * TOP))
        attended = jnp.concatenate(halves, axis=0)
        squares += jnp.sum(attended * attended, axis=1, keepdims=True)
        gate = jnp.sum(jnp.where(picked, gate_ref[:, cols], 0.0), axis=0, keepdims=True)
        gated_ref[:, cols] = attended * gate
    row = lax.broadcasted_iota(I32, (ROWS, DIM), 0)
    column = lax.broadcasted_iota(I32, (ROWS, DIM), 1)
    line = jnp.sum(jnp.where(row == column, squares, 0.0), axis=0, keepdims=True)
    square_ref[...] = jnp.broadcast_to(line[None], square_ref.shape)


def merge(timestep, msg, gate):
    smem = pl.BlockSpec(memory_space=pltpu.SMEM)
    vmem = pl.BlockSpec(memory_space=pltpu.VMEM)
    return pl.pallas_call(
        merge_kernel,
        in_specs=[smem, vmem, vmem],
        out_specs=[vmem, vmem],
        out_shape=[
            jax.ShapeDtypeStruct((ROWS, WIDTH), F32),
            jax.ShapeDtypeStruct((8, 1, DIM), F32),
        ],
        compiler_params=pltpu.CompilerParams(vmem_limit_bytes=40 * 2**20),
        name="merge",
    )(timestep, msg, gate)


def evict_kernel(owner_ref, evictor_ref, *refs):
    blocks, (nk_ref, nv_ref, held, sem) = refs[: len(TURNS)], refs[-4:]

    @pl.when(owner_ref[0] == evictor_ref[0])
    def _():
        fetches = [
            pltpu.make_async_copy(block, held.at[at], sem.at[at]) for at, block in enumerate(blocks)
        ]
        for fetch in fetches:
            fetch.start()
        for fetch in fetches:
            fetch.wait()
        copies = []
        for at, turn in enumerate(TURNS):
            x = ((owner_ref[0] >> 1) & 3) ^ turn
            for half, out_ref in enumerate((nk_ref, nv_ref)):
                copies.append(
                    pltpu.make_async_copy(
                        held.at[at, :, :, half * WIDTH : (half + 1) * WIDTH],
                        out_ref.at[:, x],
                        sem.at[len(TURNS) + 2 * at + half],
                    )
                )
        for copy in copies:
            copy.start()
        for copy in copies:
            copy.wait()


def evict(owner, evictor, blocks, next_key, next_value):
    smem = pl.BlockSpec(memory_space=pltpu.SMEM)
    hbm = pl.BlockSpec(memory_space=pl.ANY)
    rows = SPLIT["yh"] * ROWS
    gathered = (SPLIT["z"], rows, 2 * WIDTH)
    cached = (SPLIT["z"], SPLIT["x"], rows, WIDTH)
    shape = jax.ShapeDtypeStruct(cached, BF16)
    first = 2 + len(TURNS)
    outs = pl.pallas_call(
        evict_kernel,
        in_specs=[smem, smem] + [hbm] * (len(TURNS) + 2),
        out_specs=[hbm, hbm],
        out_shape=[shape, shape],
        input_output_aliases={first: 0, first + 1: 1},
        scratch_shapes=[
            pltpu.VMEM((len(TURNS),) + gathered, BF16),
            pltpu.SemaphoreType.DMA((3 * len(TURNS),)),
        ],
        compiler_params=pltpu.CompilerParams(vmem_limit_bytes=60 * 2**20),
        name="evict",
    )(
        owner,
        evictor,
        *[block.reshape(gathered) for block in blocks],
        next_key.reshape(cached),
        next_value.reshape(cached),
    )
    return [out.reshape(CACHE, WIDTH) for out in outs]


def pick_kernel(sheet_ref, after_ref, kv_ref):
    kv_ref[...] = sheet_ref[:, WIDTH:]


def pick(sheet, after):
    vmem = pl.BlockSpec(memory_space=pltpu.VMEM)
    return pl.pallas_call(
        pick_kernel,
        in_specs=[vmem, pl.BlockSpec(memory_space=pl.ANY)],
        out_specs=vmem,
        out_shape=jax.ShapeDtypeStruct((sheet.shape[0], 2 * WIDTH), BF16),
        name="pick",
    )(sheet, after)


def spread(block, axis):
    copies = math.prod(SPLIT[name] for name in (axis if isinstance(axis, tuple) else (axis,)))
    sent = jnp.broadcast_to(block[None], (copies,) + block.shape)
    return lax.all_to_all(sent, axis, 0, 0, tiled=True)


def around(block):
    ways = [[(i, i ^ turn) for i in range(SPLIT["x"])] for turn in TURNS[1:]]
    return [block] + [lax.ppermute(block, "x", way) for way in ways]


def body(
    fresh_query,
    fresh_key,
    fresh_value,
    cache_key,
    cache_value,
    slot_owner,
    evictor,
    timestep,
    age_slope,
    time_gate,
):
    owner = lax.axis_index(CTX).astype(I32).reshape(1)
    fresh = jnp.concatenate([fresh_query, fresh_key, fresh_value], axis=1)
    sheet = spread(fresh, SHEET).reshape(-1, 3 * WIDTH)
    queries = around(sheet[:, :WIDTH])
    slope = age_slope.reshape(1, HEADS)
    cache = (cache_key, cache_value, sheet, slot_owner.reshape(1, OWNERS))
    msg, next_key, next_value = attend(TURNS[:1], owner, slope, queries[:1], *cache)
    (msg,) = attend(TURNS[1:], owner, slope, queries[1:], *cache, msg)
    kv = around(pick(sheet, msg))
    msg = lax.all_to_all(msg, ("x",) + SHEET, 0, 0, tiled=True)
    gated, squares = merge(timestep, msg, time_gate)
    squares = lax.all_to_all(squares, HEAD, 0, 0, tiled=True)
    next_key, next_value = evict(owner, evictor, kv, next_key, next_value)
    squares = jnp.sum(squares, axis=(0, 1))[:ROWS, None]
    attn_output = (gated * lax.rsqrt(squares / FEATURES + 1e-06)).astype(BF16)
    return attn_output, next_key, next_value


def solution(mesh):
    split = Mesh(mesh.devices.reshape(tuple(SPLIT.values())), tuple(SPLIT))
    both = P(CTX, HEAD)
    return jax.shard_map(
        body,
        mesh=split,
        in_specs=(both,) * 5 + (P(), P(), P(), P(HEAD), P(None, HEAD)),
        out_specs=(both, both, both),
        check_vma=False,
    )
```
